32 devices in a mesh: seq: 8 (over z, x), layer: 4 (over y, core).
Axes of the slice: x: 2, y: 2, z: 4, core: 2. Of those that a mesh axis runs over, the one named last changes fastest.
Arguments:
- train_inputs: bfloat16 [4, 1024, 4096], P('layer', 'seq'), may hold values from -6 to 6
- out_grads: bfloat16 [4, 1024, 14336], P('layer', 'seq'), may hold values from -6 to 6
- query_blocks: bfloat16 [4, 14336, 4096], P('layer', 'seq'), may hold values from -0.00036621094 to 0.00036621094
- basis_in: bfloat16 [4, 32, 128, 128], P('layer'), may hold values from -0.5 to 0.5
- basis_out: bfloat16 [4, 112, 128, 128], P('layer', 'seq'), may hold values from -0.5 to 0.5
- block_of: int32 [4, 8], P('layer'), may hold values from 0 to 7, each once within a row
Outputs:
- scores: float32 [1024], P('seq')
The draws below stay inside these ranges and needn't reach their ends.
Inputs may be any that keep to these rules, and one draw needn't show every extreme that they name: Each row of block_of names every eigenbasis block of its layer once.
All inputs are finite; a program needn't handle non-finite values.
Results may differ from the reference program's by a relative error of at most 0.0055.
Values may be sent and summed in bfloat16 or wider, within the bound.
No kernel may reach another device: no remote copies, remote signals or barrier semaphores. Data moves between devices by JAX's collectives and lax.ppermute only.
A program may use at most 128 MiB of HBM per device.

```python
import jax
import jax.numpy as jnp
from jax import lax

D_IN = 4096
D_OUT = 14336
RB = 128
TOKENS = 1024
LAYERS = 4
NBLK = 8


def steps_of(own_key, shape, cuts, least, high):
    level = 1.0
    for dim, blocks in cuts:
        heights = jax.random.uniform(jax.random.fold_in(jax.random.fold_in(own_key, 6), dim), (blocks,), jnp.float32, least / len(cuts), high / len(cuts))
        level = level * jnp.repeat(jnp.exp(heights), shape[dim] // blocks).reshape((-1,) + (1,) * (len(shape) - 1 - dim))
    return level


def gaussian(own_key, shape, spread, reach, pieces=(), dtype=jnp.bfloat16):
    entries = spread * jax.random.normal(own_key, shape, jnp.float32)
    if pieces:
        entries = entries * steps_of(own_key, shape, pieces, -0.22, 0.18)
    return jnp.clip(entries, -reach, reach).astype(dtype)


def setup_inputs(seed: int = 0) -> dict:
    key_of = jax.random.split(jax.random.key(seed), 7)
    return {
        "train_inputs": gaussian(key_of[0], (LAYERS, TOKENS, D_IN), 1.0, 6.0, ((0, 4), (1, 8))),
        "out_grads": gaussian(key_of[1], (LAYERS, TOKENS, D_OUT), 1.0, 6.0, ((0, 4), (1, 8))),
        "query_blocks": gaussian(key_of[2], (LAYERS, D_OUT, D_IN), (LAYERS * D_OUT * D_IN) ** -0.5, 0.00036621094, ((0, 4), (1, 8))),
        "basis_in": gaussian(key_of[3], (LAYERS, D_IN // RB, RB, RB), RB ** -0.5, 0.5, ((0, 4),)),
        "basis_out": gaussian(key_of[4], (LAYERS, D_OUT // RB, RB, RB), RB ** -0.5, 0.5, ((0, 4), (1, 8))),
        "block_of": jax.vmap(lambda own: jax.random.permutation(own, NBLK))(jax.random.split(key_of[5], LAYERS)).reshape((LAYERS, NBLK)).astype(jnp.int32),
    }


def turn_rows(rows, basis):
    count = rows.shape[0]
    groups = rows.reshape(count, basis.shape[0], basis.shape[1]).astype(jnp.float32)
    turned = jnp.einsum('tnr,nrs->tns', groups, basis.astype(jnp.float32))
    return turned.reshape(count, -1).astype(jnp.bfloat16)


def reference(train_inputs, out_grads, query_blocks, basis_in, basis_out, block_of):
    def one_layer(total, items):
        acts, grads, query, rot_in, rot_out, owners = items
        count = acts.shape[0]
        rotated = turn_rows(acts, rot_in)
        picked = jnp.take(grads.reshape(count, owners.shape[0], -1), owners.astype(jnp.int32), axis=1)
        turned = turn_rows(picked.reshape(count, -1), rot_out)
        projected = lax.dot_general(rotated, query, (((1,), (1,)), ((), ())), preferred_element_type=jnp.float32)
        return total + jnp.sum(projected * turned.astype(jnp.float32), axis=1), None

    start_total = jnp.zeros((train_inputs.shape[1],), jnp.float32)
    total, _ = lax.scan(one_layer, start_total, (train_inputs, out_grads, query_blocks, basis_in, basis_out, block_of))
    return total
```

```python
import functools

import jax
import jax.numpy as jnp
from jax import lax
from jax.experimental import pallas as pl
from jax.experimental.pallas import tpu as pltpu
from jax.sharding import PartitionSpec as P

LINE = 4
TILE = 128
NT = (((1,), (1,)), ((), ()))
hold = lax.optimization_barrier


def project_kernel(count, *refs):
    chunks, (basis, query, out, turned) = refs[:count], refs[count:]
    rows, order = chunks[0].shape[0], basis.shape[1]

    @pl.when(pl.program_id(0) == 0)
    def _():
        for c, chunk in enumerate(chunks):
            for n in range(basis.shape[0]):
                part = pl.ds(n * order, order)
                turned[pl.ds(c * rows, rows), part] = jnp.dot(
                    chunk[:, part], basis[n], preferred_element_type=jnp.float32
                ).astype(jnp.bfloat16)

    found = lax.dot_general(turned[...], query[...], NT, preferred_element_type=jnp.float32)
    out[...] = found.reshape(out.shape)


def project(chunks, basis, query):
    count, (rows, wide) = len(chunks), chunks[0].shape
    units = query.shape[0]
    step = 2 * TILE if units % (2 * TILE) == 0 else TILE
    whole = lambda *shape: pl.BlockSpec(shape, lambda i: (0,) * len(shape))
    return pl.pallas_call(
        functools.partial(project_kernel, count),
        grid=(units // step,),
        in_specs=[whole(rows, wide)] * count + [whole(*basis.shape), pl.BlockSpec((step, wide), lambda i: (i, 0))],
        out_specs=pl.BlockSpec((count, rows, step), lambda i: (0, 0, i)),
        out_shape=jax.ShapeDtypeStruct((count, rows, units), jnp.float32),
        scratch_shapes=[pltpu.VMEM((count * rows, wide), jnp.bfloat16)],
        compiler_params=pltpu.CompilerParams(vmem_limit_bytes=24 * 2**20),
        cost_estimate=pl.CostEstimate(
            flops=2 * count * rows * wide * (units + TILE), bytes_accessed=2 * wide * units, transcendentals=0
        ),
    )(*chunks, basis, query)


def score_kernel(pick, first, second, piece, basis, out):
    order = basis.shape[1]
    total = jnp.zeros((piece.shape[0], order), jnp.float32)
    for n in range(basis.shape[0]):
        part = pl.ds(n * order, order)
        turned = jnp.dot(piece[:, part], basis[n], preferred_element_type=jnp.float32).astype(jnp.bfloat16)
        held = jnp.where(pick[0] == 1, first[:, part], second[:, part])
        total += turned.astype(jnp.float32) * held
    out[...] = jnp.sum(total.T, axis=0, keepdims=True)


def score(pick, first, second, piece, basis):
    vmem = pl.BlockSpec(memory_space=pltpu.VMEM)
    return pl.pallas_call(
        score_kernel,
        in_specs=[pl.BlockSpec(memory_space=pltpu.SMEM)] + [vmem] * 4,
        out_specs=vmem,
        out_shape=jax.ShapeDtypeStruct((1, piece.shape[0]), jnp.float32),
        compiler_params=pltpu.CompilerParams(vmem_limit_bytes=16 * 2**20),
    )(pick, first, second, piece, basis)


def body(across, train_inputs, out_grads, query_blocks, basis_in, basis_out, block_of):
    own, grads, query = train_inputs[0], out_grads[0], query_blocks[0]
    turn_in, turn_out, owners = basis_in[0], basis_out[0], block_of[0]
    size, units = LINE * across, query.shape[0]
    me = lax.axis_index("seq")
    inner = (me // across == 1) | (me // across == 2)
    pick = inner.astype(jnp.int32).reshape(1)

    def move(value, place):
        pairs = []
        for s in range(size):
            to = place(s // across, s % across)
            if to is not None:
                pairs.append((s, to[0] * across + to[1]))
        return lax.ppermute(value, "seq", pairs)

    def swap(value, j):
        return lax.ppermute(value, "seq", [(s, s ^ j) for s in range(size)])

    def sideways(value):
        return [swap(value, j) for j in range(1, across)]

    middle = lambda value: move(value, lambda z, x: (3 - z, x) if z in (1, 2) else None)
    inward = lambda value: move(value, lambda z, x: (z ^ 1, x) if z in (1, 2) else None)
    line = lambda value, d: swap(value, d * across)
    piece_for = lambda j: lax.dynamic_slice_in_dim(grads, owners[me ^ j] * units, units, axis=1)
    send = lambda pieces, js: {j: swap(pieces[j], j) for j in js}
    aside = lambda d: [d * across + j for j in range(1, across)]

    a1, a2, a3 = line(own, 1), middle(own), sideways(own)
    pieces = {j: piece_for(j) for j in range(size)}
    p_own = project([own], turn_in, query)
    a1, a2, a3, pieces, p_own = hold((a1, a2, a3, pieces, p_own))
    b1, b2, b3 = middle(a1), inward(a2), sideways(a1)
    p_a = project([a1] + a3, turn_in, query)
    r0 = score(pick, p_own[0], p_own[0], pieces[0], turn_out)
    b1, b2, b3, pieces, p_a, r0 = hold((b1, b2, b3, pieces, p_a, r0))
    c1 = inward(b1)
    near = jnp.where(inner, a2, b2)
    near_side = sideways(near)
    got = send(pieces, aside(2) + [3 * across] + aside(0))
    p_b = project([near] + b3, turn_in, query)
    c1, near_side, got, pieces, p_b = hold((c1, near_side, got, pieces, p_b))
    far = jnp.where(inner, b1, c1)
    far_side = sideways(far)
    got.update(send(pieces, [2 * across] + aside(3) + aside(1) + [across]))
    p_c = project([far] + near_side, turn_in, query)
    scores = {0: r0}
    for j in range(1, across):
        scores[j] = score(pick, p_a[j], p_a[j], got[j], turn_out)
    scores, far_side, got, p_c = hold((scores, far_side, got, p_c))
    p_d = project(far_side, turn_in, query)
    scores[across] = score(pick, p_a[0], p_a[0], got[across], turn_out)
    scores[2 * across] = score(pick, p_c[0], p_b[0], got[2 * across], turn_out)
    scores[3 * across] = score(pick, p_b[0], p_c[0], got[3 * across], turn_out)
    for j in range(1, across):
        scores[across + j] = score(pick, p_b[j], p_b[j], got[across + j], turn_out)
        scores[2 * across + j] = score(pick, p_d[j - 1], p_c[j], got[2 * across + j], turn_out)
        scores[3 * across + j] = score(pick, p_c[j], p_d[j - 1], got[3 * across + j], turn_out)
    partial = jnp.concatenate([scores[j] for j in range(size)], axis=0)
    partial = jnp.take(partial, jnp.arange(size) ^ me, axis=0)
    share = jnp.sum(lax.all_to_all(partial, "seq", split_axis=0, concat_axis=0, tiled=True), axis=0)
    return lax.psum(share, "layer")


def solution(mesh):
    placed = (
        P("layer", "seq", None),
        P("layer", "seq", None),
        P("layer", "seq", None),
        P("layer", None, None, None),
        P("layer", "seq", None, None),
        P("layer", None),
    )
    across = mesh.shape["seq"] // LINE
    return jax.shard_map(
        functools.partial(body, across), mesh=mesh, in_specs=placed, out_specs=P("seq"), check_vma=False
    )
```

```python
import functools

import jax
import jax.numpy as jnp
from jax import lax
from jax.experimental import pallas as pl
from jax.experimental.pallas import tpu as pltpu
from jax.sharding import PartitionSpec as P

LINE = 4
TILE = 128
NT = (((1,), (1,)), ((), ()))
hold = lax.optimization_barrier


def project_kernel(count, *refs):
    chunks, (basis, query, out, turned) = refs[:count], refs[count:]
    rows, order = chunks[0].shape[0], basis.shape[1]

    @pl.when(pl.program_id(0) == 0)
    def _():
        for c, chunk in enumerate(chunks):
            for n in range(basis.shape[0]):
                part = pl.ds(n * order, order)
                turned[pl.ds(c * rows, rows), part] = jnp.dot(
                    chunk[:, part], basis[n], preferred_element_type=jnp.float32
                ).astype(jnp.bfloat16)

    found = lax.dot_general(turned[...], query[...], NT, preferred_element_type=jnp.float32)
    out[...] = found.reshape(out.shape)


def project(chunks, basis, query):
    count, (rows, wide) = len(chunks), chunks[0].shape
    units = query.shape[0]
    step = 2 * TILE if units % (2 * TILE) == 0 else TILE
    whole = lambda *shape: pl.BlockSpec(shape, lambda i: (0,) * len(shape))
    return pl.pallas_call(
        functools.partial(project_kernel, count),
        grid=(units // step,),
        in_specs=[whole(rows, wide)] * count + [whole(*basis.shape), pl.BlockSpec((step, wide), lambda i: (i, 0))],
        out_specs=pl.BlockSpec((count, rows, step), lambda i: (0, 0, i)),
        out_shape=jax.ShapeDtypeStruct((count, rows, units), jnp.float32),
        scratch_shapes=[pltpu.VMEM((count * rows, wide), jnp.bfloat16)],
        compiler_params=pltpu.CompilerParams(vmem_limit_bytes=24 * 2**20),
        cost_estimate=pl.CostEstimate(
            flops=2 * count * rows * wide * (units + TILE), bytes_accessed=2 * wide * units, transcendentals=0
        ),
    )(*chunks, basis, query)


def score_kernel(pick, first, second, piece, basis, out):
    order = basis.shape[1]
    total = jnp.zeros((piece.shape[0], order), jnp.float32)
    for n in range(basis.shape[0]):
        part = pl.ds(n * order, order)
        turned = jnp.dot(piece[:, part], basis[n], preferred_element_type=jnp.float32).astype(jnp.bfloat16)
        held = jnp.where(pick[0] == 1, first[:, part], second[:, part])
        total += turned.astype(jnp.float32) * held
    out[...] = jnp.sum(total.T, axis=0, keepdims=True)


def score(pick, first, second, piece, basis):
    vmem = pl.BlockSpec(memory_space=pltpu.VMEM)
    return pl.pallas_call(
        score_kernel,
        in_specs=[pl.BlockSpec(memory_space=pltpu.SMEM)] + [vmem] * 4,
        out_specs=vmem,
        out_shape=jax.ShapeDtypeStruct((1, piece.shape[0]), jnp.float32),
        compiler_params=pltpu.CompilerParams(vmem_limit_bytes=16 * 2**20),
    )(pick, first, second, piece, basis)


def back_kernel(found, basis, out):
    order = basis.shape[1]
    for n in range(basis.shape[0]):
        part = pl.ds(n * order, order)
        held = found[:, part]
        high = held.astype(jnp.bfloat16)
        low = (held - high.astype(jnp.float32)).astype(jnp.bfloat16)
        turned = lax.dot_general(high, basis[n], NT, preferred_element_type=jnp.float32)
        turned += lax.dot_general(low, basis[n], NT, preferred_element_type=jnp.float32)
        out[:, part] = turned.astype(jnp.bfloat16)


def back(found, basis):
    vmem = pl.BlockSpec(memory_space=pltpu.VMEM)
    return pl.pallas_call(
        back_kernel,
        in_specs=[vmem] * 2,
        out_specs=vmem,
        out_shape=jax.ShapeDtypeStruct(found.shape, jnp.bfloat16),
        compiler_params=pltpu.CompilerParams(vmem_limit_bytes=16 * 2**20),
    )(found, basis)


def meet_kernel(count, *refs):
    out = refs[-1]
    total = jnp.zeros((refs[0].shape[0], TILE), jnp.float32)
    for c in range(count):
        for n in range(refs[c].shape[1] // TILE):
            part = pl.ds(n * TILE, TILE)
            total += refs[c][:, part].astype(jnp.float32) * refs[count + c][:, part].astype(jnp.float32)
    out[...] = jnp.sum(total.T, axis=0, keepdims=True)


def meet(lefts, rights):
    vmem = pl.BlockSpec(memory_space=pltpu.VMEM)
    return pl.pallas_call(
        functools.partial(meet_kernel, len(lefts)),
        in_specs=[vmem] * (2 * len(lefts)),
        out_specs=vmem,
        out_shape=jax.ShapeDtypeStruct((1, lefts[0].shape[0]), jnp.float32),
        compiler_params=pltpu.CompilerParams(vmem_limit_bytes=16 * 2**20),
    )(*lefts, *rights)


def body(across, train_inputs, out_grads, query_blocks, basis_in, basis_out, block_of):
    own, grads, query = train_inputs[0], out_grads[0], query_blocks[0]
    turn_in, turn_out, owners = basis_in[0], basis_out[0], block_of[0]
    size, units = LINE * across, query.shape[0]
    me = lax.axis_index("seq")
    inner = (me // across == 1) | (me // across == 2)
    pick = inner.astype(jnp.int32).reshape(1)

    def move(value, place):
        pairs = []
        for s in range(size):
            to = place(s // across, s % across)
            if to is not None:
                pairs.append((s, to[0] * across + to[1]))
        return lax.ppermute(value, "seq", pairs)

    def swap(value, j):
        return lax.ppermute(value, "seq", [(s, s ^ j) for s in range(size)])

    def sideways(value):
        return [swap(value, j) for j in range(1, across)]

    middle = lambda value: move(value, lambda z, x: (3 - z, x) if z in (1, 2) else None)
    inward = lambda value: move(value, lambda z, x: (z ^ 1, x) if z in (1, 2) else None)
    line = lambda value, d: swap(value, d * across)
    piece_for = lambda j: lax.dynamic_slice_in_dim(grads, owners[me ^ j] * units, units, axis=1)
    send = lambda values: {j: swap(value, j) for j, value in values.items()}
    aside = lambda d: [d * across + j for j in range(1, across)]
    forward = aside(2) + aside(3)

    a1, a2, a3 = line(own, 1), middle(own), sideways(own)
    pieces = {j: piece_for(j) for j in range(size)}
    p_own = project([own], turn_in, query)
    a1, a2, a3, pieces, p_own = hold((a1, a2, a3, pieces, p_own))
    b1, b2, b3 = middle(a1), inward(a2), sideways(a1)
    p_a = project([a1] + a3, turn_in, query)
    total = score(pick, p_own[0], p_own[0], pieces[0], turn_out)
    b1, b2, b3, pieces, p_a, total = hold((b1, b2, b3, pieces, p_a, total))
    c1 = inward(b1)
    near = jnp.where(inner, a2, b2)
    near_side = sideways(near)
    got = send({j: pieces[j] for j in forward})
    p_b = project([near] + b3, turn_in, query)
    ready = {across: back(p_a[0], turn_out)}
    for j in range(1, across):
        ready[j] = back(p_a[j], turn_out)
        ready[across + j] = back(p_b[j], turn_out)
    c1, near_side, got, pieces, p_b, ready = hold((c1, near_side, got, pieces, p_b, ready))
    far = jnp.where(inner, b1, c1)
    far_side = sideways(far)
    got[3 * across] = swap(pieces[3 * across], 3 * across)
    come = {across: swap(ready[across], across)}
    p_c = project([far] + near_side, turn_in, query)
    come[2 * across] = swap(back(jnp.where(inner, p_c[0], p_b[0]), turn_out), 2 * across)
    far_side, late, p_c = hold((far_side, {j: ready[j] for j in aside(0) + aside(1)}, p_c))
    come.update(send(late))
    p_d = project(far_side, turn_in, query)
    sums = {3 * across: score(pick, p_b[0], p_c[0], got[3 * across], turn_out)}
    for j in range(1, across):
        sums[2 * across + j] = score(pick, p_d[j - 1], p_c[j], got[2 * across + j], turn_out)
        sums[3 * across + j] = score(pick, p_c[j], p_d[j - 1], got[3 * across + j], turn_out)
    for value in send(sums).values():
        total += value
    first = [across, 2 * across]
    total += meet([come[j] for j in first], [pieces[j] for j in first])
    total, late = hold((total, {j: come[j] for j in late}))
    total += meet(list(late.values()), [pieces[j] for j in late])
    return lax.psum(total[0], "layer")


def solution(mesh):
    placed = (
        P("layer", "seq", None),
        P("layer", "seq", None),
        P("layer", "seq", None),
        P("layer", None, None, None),
        P("layer", "seq", None, None),
        P("layer", None),
    )
    across = mesh.shape["seq"] // LINE
    return jax.shard_map(
        functools.partial(body, across), mesh=mesh, in_specs=placed, out_specs=P("seq"), check_vma=False
    )
```

```python
import functools

import jax
import jax.numpy as jnp
from jax import lax
from jax.experimental import pallas as pl
from jax.experimental.pallas import tpu as pltpu
from jax.sharding import PartitionSpec as P

LINE = 4
TILE = 128
MIB = 2**20
NT = (((1,), (1,)), ((), ()))
hold = lax.optimization_barrier
free = pl.CostEstimate(flops=0, bytes_accessed=0, transcendentals=0)


def blocks_of(wide):
    return [pl.ds(n * TILE, TILE) for n in range(wide // TILE)]


def project_kernel(count, *refs):
    chunks, (basis, query, out, turned) = refs[:count], refs[count:]
    rows = chunks[0].shape[0]

    @pl.when(pl.program_id(0) == 0)
    def _():
        for c, chunk in enumerate(chunks):
            for n, part in enumerate(blocks_of(chunk.shape[1])):
                turned[pl.ds(c * rows, rows), part] = jnp.dot(
                    chunk[:, part], basis[n], preferred_element_type=jnp.float32
                ).astype(jnp.bfloat16)

    found = lax.dot_general(turned[...], query[...], NT, preferred_element_type=jnp.float32)
    out[...] = found.reshape(out.shape)


def project(chunks, basis, query):
    count, (rows, wide) = len(chunks), chunks[0].shape
    units = query.shape[0]
    step = 2 * TILE if units % (2 * TILE) == 0 else TILE
    whole = lambda *shape: pl.BlockSpec(shape, lambda i: (0,) * len(shape))
    return pl.pallas_call(
        functools.partial(project_kernel, count),
        grid=(units // step,),
        in_specs=[whole(rows, wide)] * count + [whole(*basis.shape), pl.BlockSpec((step, wide), lambda i: (i, 0))],
        out_specs=pl.BlockSpec((count, rows, step), lambda i: (0, 0, i)),
        out_shape=jax.ShapeDtypeStruct((count, rows, units), jnp.float32),
        scratch_shapes=[pltpu.VMEM((count * rows, wide), jnp.bfloat16)],
        compiler_params=pltpu.CompilerParams(vmem_limit_bytes=50 * MIB),
        cost_estimate=free,
    )(*chunks, basis, query)


def pack_kernel(count, order, *refs):
    for piece, out in zip(refs[:count], refs[count:]):
        out[...] = piece[...]


def pack(offsets, order, grads, units):
    rows, count = grads.shape[0], len(offsets)
    found = pl.pallas_call(
        functools.partial(pack_kernel, count),
        grid_spec=pltpu.PrefetchScalarGridSpec(
            num_scalar_prefetch=1,
            grid=(1,),
            in_specs=[pl.BlockSpec((rows, units), lambda i, order, j=j: (0, order[j])) for j in offsets],
            out_specs=[pl.BlockSpec((rows, units), lambda i, order: (0, 0))] * count,
        ),
        out_shape=[jax.ShapeDtypeStruct((rows, units), grads.dtype)] * count,
        compiler_params=pltpu.CompilerParams(vmem_limit_bytes=16 * MIB),
        cost_estimate=free,
    )(order, *[grads] * count)
    return dict(zip(offsets, found))


def lay(total):
    return jnp.sum(total.T, axis=0, keepdims=True)


def score_kernel(order, found, piece, basis, out):
    total = jnp.zeros((piece.shape[0], TILE), jnp.float32)
    for n, part in enumerate(blocks_of(piece.shape[1])):
        turned = jnp.dot(piece[:, part], basis[n], preferred_element_type=jnp.float32).astype(jnp.bfloat16)
        total += turned.astype(jnp.float32) * found[:, part]
    out[...] = lay(total)


def meet_kernel(count, order, *refs):
    total = jnp.zeros((refs[0].shape[0], TILE), jnp.float32)
    for came, piece in zip(refs[:count], refs[count:-1]):
        for part in blocks_of(piece.shape[1]):
            total += came[:, part].astype(jnp.float32) * piece[:, part].astype(jnp.float32)
    refs[-1][...] = lay(total)


def small(kernel, order, in_specs, rows, *args):
    return pl.pallas_call(
        kernel,
        grid_spec=pltpu.PrefetchScalarGridSpec(
            num_scalar_prefetch=1,
            grid=(1,),
            in_specs=in_specs,
            out_specs=pl.BlockSpec((1, rows), lambda i, order: (0, 0)),
        ),
        out_shape=jax.ShapeDtypeStruct((1, rows), jnp.float32),
        compiler_params=pltpu.CompilerParams(vmem_limit_bytes=16 * MIB),
        cost_estimate=free,
    )(order, *args)


def score(found, c, order, j, values, basis):
    _, rows, units = found.shape
    at = (lambda i, order: (0, 0)) if j is None else (lambda i, order: (0, order[j]))
    specs = [
        pl.BlockSpec((None, rows, units), lambda i, order: (c, 0, 0)),
        pl.BlockSpec((rows, units), at),
        pl.BlockSpec(basis.shape, lambda i, order: (0, 0, 0)),
    ]
    return small(score_kernel, order, specs, rows, found, values, basis)


def meet(come, order, grads):
    offsets = list(come)
    rows, units = come[offsets[0]].shape
    specs = [pl.BlockSpec((rows, units), lambda i, order: (0, 0))] * len(offsets)
    specs += [pl.BlockSpec((rows, units), lambda i, order, j=j: (0, order[j])) for j in offsets]
    args = [come[j] for j in offsets] + [grads] * len(offsets)
    return small(functools.partial(meet_kernel, len(offsets)), order, specs, rows, *args)


def back_kernel(found, basis, out):
    for n, part in enumerate(blocks_of(found.shape[1])):
        held = found[:, part]
        high = held.astype(jnp.bfloat16)
        low = (held - high.astype(jnp.float32)).astype(jnp.bfloat16)
        turned = lax.dot_general(high, basis[n], NT, preferred_element_type=jnp.float32)
        turned += lax.dot_general(low, basis[n], NT, preferred_element_type=jnp.float32)
        out[:, part] = turned.astype(jnp.bfloat16)


def back(found, c, basis):
    _, rows, units = found.shape
    return pl.pallas_call(
        back_kernel,
        grid=(1,),
        in_specs=[
            pl.BlockSpec((None, rows, units), lambda i: (c, 0, 0)),
            pl.BlockSpec(basis.shape, lambda i: (0, 0, 0)),
        ],
        out_specs=pl.BlockSpec((rows, units), lambda i: (0, 0)),
        out_shape=jax.ShapeDtypeStruct((rows, units), jnp.bfloat16),
        compiler_params=pltpu.CompilerParams(vmem_limit_bytes=16 * MIB),
        cost_estimate=free,
    )(found, basis)


def body(across, train_inputs, out_grads, query_blocks, basis_in, basis_out, block_of):
    own, grads, query = train_inputs[0], out_grads[0], query_blocks[0]
    turn_in, turn_out, owners = basis_in[0], basis_out[0], block_of[0]
    size, units = LINE * across, query.shape[0]
    me = lax.axis_index("seq")
    inner = (me // across == 1) | (me // across == 2)
    order = jnp.take(owners, jnp.arange(size) ^ me)

    def move(value, place):
        pairs = []
        for s in range(size):
            to = place(s // across, s % across)
            if to is not None:
                pairs.append((s, to[0] * across + to[1]))
        return lax.ppermute(value, "seq", pairs)

    def swap(value, j):
        return lax.ppermute(value, "seq", [(s, s ^ j) for s in range(size)])

    def sideways(value):
        return [swap(value, j) for j in range(1, across)]

    middle = lambda value: move(value, lambda z, x: (3 - z, x) if z in (1, 2) else None)
    inward = lambda value: move(value, lambda z, x: (z ^ 1, x) if z in (1, 2) else None)
    line = lambda value, d: swap(value, d * across)
    send = lambda values, js: {j: swap(values[j], j) for j in js}
    aside = lambda d: [d * across + j for j in range(1, across)]
    one, two, three = across, 2 * across, 3 * across

    a1, a2, a3 = line(own, 1), middle(own), sideways(own)
    pieces = pack([three] + aside(3), order, grads, units)
    p_own = project([own], turn_in, query)
    a1, pieces, p_own = hold((a1, pieces, p_own))
    b1, b3, b2 = middle(a1), sideways(a1), inward(a2)
    p_a = project([a1] + a3, turn_in, query)
    total = score(p_own, 0, order, 0, grads, turn_out)
    ready = {one: back(p_a, 0, turn_out)}
    for j in range(1, across):
        ready[j] = back(p_a, j, turn_out)
    a2, b1, b2, b3, pieces, total, ready = hold((a2, b1, b2, b3, pieces, total, ready))
    c1 = inward(b1)
    far2 = jnp.where(inner, b1, b2)
    side2 = sideways(far2)
    got = send(pieces, [three] + aside(3))
    come = send(ready, aside(0))
    p_b = project([far2] + b3, turn_in, query)
    ready[two] = back(p_b, 0, turn_out)
    for j in range(1, across):
        ready[one + j] = back(p_b, j, turn_out)
    c1, side2, got, come, ready = hold((c1, side2, got, come, ready))
    far3 = jnp.where(inner, a2, c1)
    side3 = sideways(far3)
    come.update(send(ready, [two, one]))
    p_c = project([far3] + side2, turn_in, query)
    sums = {three: score(p_c, 0, order, None, got[three], turn_out)}
    for j in range(1, across):
        ready[two + j] = back(p_c, j, turn_out)
    total += meet({j: come[j] for j in aside(0)}, order, grads)
    side3, ready, total = hold((side3, ready, total))
    late = aside(2) + aside(1)
    come.update(send(ready, late))
    p_d = project(side3, turn_in, query)
    for j in range(1, across):
        sums[three + j] = score(p_d, j - 1, order, None, got[three + j], turn_out)
    for value in send(sums, list(sums)).values():
        total += value
    total += meet({j: come[j] for j in (two, one)}, order, grads)
    total, come = hold((total, come))
    total += meet({j: come[j] for j in late}, order, grads)
    return lax.psum(total[0], "layer")


def solution(mesh):
    placed = (
        P("layer", "seq", None),
        P("layer", "seq", None),
        P("layer", "seq", None),
        P("layer", None, None, None),
        P("layer", "seq", None, None),
        P("layer", None),
    )
    across = mesh.shape["seq"] // LINE
    return jax.shard_map(
        functools.partial(body, across), mesh=mesh, in_specs=placed, out_specs=P("seq"), check_vma=False
    )
```

```python
import functools

import jax
import jax.numpy as jnp
from jax import lax
from jax.experimental import pallas as pl
from jax.experimental.pallas import tpu as pltpu
from jax.sharding import PartitionSpec as P

LINE = 4
TILE = 128
MIB = 2**20
NT = (((1,), (1,)), ((), ()))
hold = lax.optimization_barrier
free = pl.CostEstimate(flops=0, bytes_accessed=0, transcendentals=0)


def blocks_of(wide):
    return [pl.ds(n * TILE, TILE) for n in range(wide // TILE)]


def project_kernel(count, *refs):
    chunks, (basis, query, out, turned) = refs[:count], refs[count:]
    rows = chunks[0].shape[0]

    @pl.when(pl.program_id(0) == 0)
    def _():
        for c, chunk in enumerate(chunks):
            for n, part in enumerate(blocks_of(chunk.shape[1])):
                turned[pl.ds(c * rows, rows), part] = jnp.dot(
                    chunk[:, part], basis[n], preferred_element_type=jnp.float32
                ).astype(jnp.bfloat16)

    found = lax.dot_general(turned[...], query[...], NT, preferred_element_type=jnp.float32)
    out[...] = found.reshape(out.shape)


def project(chunks, basis, query):
    count, (rows, wide) = len(chunks), chunks[0].shape
    units = query.shape[0]
    step = 2 * TILE if units % (2 * TILE) == 0 else TILE
    whole = lambda *shape: pl.BlockSpec(shape, lambda i: (0,) * len(shape))
    return pl.pallas_call(
        functools.partial(project_kernel, count),
        grid=(units // step,),
        in_specs=[whole(rows, wide)] * count + [whole(*basis.shape), pl.BlockSpec((step, wide), lambda i: (i, 0))],
        out_specs=pl.BlockSpec((count, rows, step), lambda i: (0, 0, i)),
        out_shape=jax.ShapeDtypeStruct((count, rows, units), jnp.float32),
        scratch_shapes=[pltpu.VMEM((count * rows, wide), jnp.bfloat16)],
        compiler_params=pltpu.CompilerParams(vmem_limit_bytes=20 * MIB),
        cost_estimate=free,
    )(*chunks, basis, query)


def pack_kernel(count, order, *refs):
    for piece, out in zip(refs[:count], refs[count:]):
        out[...] = piece[...]


def pack(offsets, order, grads, units):
    rows, count = grads.shape[0], len(offsets)
    found = pl.pallas_call(
        functools.partial(pack_kernel, count),
        grid_spec=pltpu.PrefetchScalarGridSpec(
            num_scalar_prefetch=1,
            grid=(1,),
            in_specs=[pl.BlockSpec((rows, units), lambda i, order, j=j: (0, order[j])) for j in offsets],
            out_specs=[pl.BlockSpec((rows, units), lambda i, order: (0, 0))] * count,
        ),
        out_shape=[jax.ShapeDtypeStruct((rows, units), grads.dtype)] * count,
        compiler_params=pltpu.CompilerParams(vmem_limit_bytes=16 * MIB),
        cost_estimate=free,
    )(order, *[grads] * count)
    return dict(zip(offsets, found))


def lay(total):
    return jnp.sum(total.T, axis=0, keepdims=True)


def score_kernel(order, found, piece, basis, out):
    total = jnp.zeros((piece.shape[0], TILE), jnp.float32)
    for n, part in enumerate(blocks_of(piece.shape[1])):
        turned = jnp.dot(piece[:, part], basis[n], preferred_element_type=jnp.float32).astype(jnp.bfloat16)
        total += turned.astype(jnp.float32) * found[:, part]
    out[...] = lay(total)


def meet_kernel(count, order, *refs):
    total = jnp.zeros((refs[0].shape[0], TILE), jnp.float32)
    for came, piece in zip(refs[:count], refs[count:-1]):
        for part in blocks_of(piece.shape[1]):
            total += came[:, part].astype(jnp.float32) * piece[:, part].astype(jnp.float32)
    refs[-1][...] = lay(total)


def small(kernel, order, in_specs, rows, *args):
    return pl.pallas_call(
        kernel,
        grid_spec=pltpu.PrefetchScalarGridSpec(
            num_scalar_prefetch=1,
            grid=(1,),
            in_specs=in_specs,
            out_specs=pl.BlockSpec((1, rows), lambda i, order: (0, 0)),
        ),
        out_shape=jax.ShapeDtypeStruct((1, rows), jnp.float32),
        compiler_params=pltpu.CompilerParams(vmem_limit_bytes=16 * MIB),
        cost_estimate=free,
    )(order, *args)


def score(found, c, order, j, values, basis):
    _, rows, units = found.shape
    at = (lambda i, order: (0, 0)) if j is None else (lambda i, order: (0, order[j]))
    specs = [
        pl.BlockSpec((None, rows, units), lambda i, order: (c, 0, 0)),
        pl.BlockSpec((rows, units), at),
        pl.BlockSpec(basis.shape, lambda i, order: (0, 0, 0)),
    ]
    return small(score_kernel, order, specs, rows, found, values, basis)


def meet(come, order, grads):
    offsets = list(come)
    rows, units = come[offsets[0]].shape
    specs = [pl.BlockSpec((rows, units), lambda i, order: (0, 0))] * len(offsets)
    specs += [pl.BlockSpec((rows, units), lambda i, order, j=j: (0, order[j])) for j in offsets]
    args = [come[j] for j in offsets] + [grads] * len(offsets)
    return small(functools.partial(meet_kernel, len(offsets)), order, specs, rows, *args)


def back_kernel(found, basis, out):
    for n, part in enumerate(blocks_of(found.shape[1])):
        held = found[:, part]
        high = held.astype(jnp.bfloat16)
        low = (held - high.astype(jnp.float32)).astype(jnp.bfloat16)
        turned = lax.dot_general(high, basis[n], NT, preferred_element_type=jnp.float32)
        turned += lax.dot_general(low, basis[n], NT, preferred_element_type=jnp.float32)
        out[:, part] = turned.astype(jnp.bfloat16)


def back(found, c, basis):
    _, rows, units = found.shape
    return pl.pallas_call(
        back_kernel,
        grid=(1,),
        in_specs=[
            pl.BlockSpec((None, rows, units), lambda i: (c, 0, 0)),
            pl.BlockSpec(basis.shape, lambda i: (0, 0, 0)),
        ],
        out_specs=pl.BlockSpec((rows, units), lambda i: (0, 0)),
        out_shape=jax.ShapeDtypeStruct((rows, units), jnp.bfloat16),
        compiler_params=pltpu.CompilerParams(vmem_limit_bytes=16 * MIB),
        cost_estimate=free,
    )(found, basis)


def project_score_kernel(chunk, basis, query, piece, turn, out, turned, total):
    @pl.when(pl.program_id(0) == 0)
    def _():
        for n, part in enumerate(blocks_of(chunk.shape[1])):
            turned[:, part] = jnp.dot(chunk[:, part], basis[n], preferred_element_type=jnp.float32).astype(jnp.bfloat16)
        total[...] = jnp.zeros_like(total)

    found = lax.dot_general(turned[...], query[...], NT, preferred_element_type=jnp.float32)
    for n in range(turn.shape[0]):
        part = slice(n * TILE, (n + 1) * TILE)
        held = jnp.dot(piece[:, part], turn[n], preferred_element_type=jnp.float32).astype(jnp.bfloat16)
        total[...] += held.astype(jnp.float32) * found[:, part]

    @pl.when(pl.program_id(0) == pl.num_programs(0) - 1)
    def _():
        out[...] = lay(total[...])


def project_score(chunk, basis, query, piece, turn):
    rows, wide = chunk.shape
    units = query.shape[0]
    step = 2 * TILE if units % (2 * TILE) == 0 else TILE
    whole = lambda *shape: pl.BlockSpec(shape, lambda i: (0,) * len(shape))
    return pl.pallas_call(
        project_score_kernel,
        grid=(units // step,),
        in_specs=[
            whole(rows, wide),
            whole(*basis.shape),
            pl.BlockSpec((step, wide), lambda i: (i, 0)),
            pl.BlockSpec((rows, step), lambda i: (0, i)),
            pl.BlockSpec((step // TILE, *turn.shape[1:]), lambda i: (i, 0, 0)),
        ],
        out_specs=whole(1, rows),
        out_shape=jax.ShapeDtypeStruct((1, rows), jnp.float32),
        scratch_shapes=[pltpu.VMEM((rows, wide), jnp.bfloat16), pltpu.VMEM((rows, TILE), jnp.float32)],
        compiler_params=pltpu.CompilerParams(vmem_limit_bytes=20 * MIB),
        cost_estimate=free,
    )(chunk, basis, query, piece, turn)


def body(across, train_inputs, out_grads, query_blocks, basis_in, basis_out, block_of):
    own, grads, query = train_inputs[0], out_grads[0], query_blocks[0]
    turn_in, turn_out, owners = basis_in[0], basis_out[0], block_of[0]
    size, units = LINE * across, query.shape[0]
    me = lax.axis_index("seq")
    inner = (me // across == 1) | (me // across == 2)
    order = jnp.take(owners, jnp.arange(size) ^ me)

    def move(value, place):
        pairs = []
        for s in range(size):
            to = place(s // across, s % across)
            if to is not None:
                pairs.append((s, to[0] * across + to[1]))
        return lax.ppermute(value, "seq", pairs)

    def swap(value, j):
        return lax.ppermute(value, "seq", [(s, s ^ j) for s in range(size)])

    def sideways(value):
        return [swap(value, j) for j in range(1, across)]

    middle = lambda value: move(value, lambda z, x: (3 - z, x) if z in (1, 2) else None)
    line = lambda value, d: swap(value, d * across)
    send = lambda values, js: {j: swap(values[j], j) for j in js}
    aside = lambda d: [d * across + j for j in range(1, across)]
    one, two, three = across, 2 * across, 3 * across

    a1, a2, a3 = line(own, 1), middle(own), sideways(own)
    pieces = pack([three] + aside(3), order, grads, units)
    p_own = project([own], turn_in, query)
    a1, pieces, p_own = hold((a1, pieces, p_own))
    got = send(pieces, aside(3))
    b1, b3, b2 = middle(a1), sideways(a1), line(a2, 1)
    p_a = project([a1] + a3, turn_in, query)
    total = score(p_own, 0, order, 0, grads, turn_out)
    ready = {one: back(p_a, 0, turn_out)}
    for j in range(1, across):
        ready[j] = back(p_a, j, turn_out)
    a2, b1, b2, b3, pieces, total, ready = hold((a2, b1, b2, b3, pieces, total, ready))
    c1 = line(b1, 1)
    far2 = jnp.where(inner, b1, b2)
    side2 = sideways(far2)
    got.update(send(pieces, [three]))
    come = send(ready, aside(0))
    p_b = project([far2] + b3, turn_in, query)
    ready[two] = back(p_b, 0, turn_out)
    for j in range(1, across):
        ready[one + j] = back(p_b, j, turn_out)
    c1, side2, got, come, ready = hold((c1, side2, got, come, ready))
    far3 = jnp.where(inner, a2, c1)
    side3 = sideways(far3)
    come.update(send(ready, [two, one]))
    p_c = project([far3] + side2, turn_in, query)
    sums = {three: score(p_c, 0, order, None, got[three], turn_out)}
    for j in range(1, across):
        ready[two + j] = back(p_c, j, turn_out)
    total += meet({j: come[j] for j in aside(0)}, order, grads)
    sums = send(sums, list(sums))
    side3, ready, total, sums = hold((side3, ready, total, sums))
    total += sums[three]
    sums = {}
    late = aside(2) + aside(1)
    come.update(send(ready, late))
    for j in range(1, across):
        sums[three + j] = project_score(side3[j - 1], turn_in, query, got[three + j], turn_out)
    for value in send(sums, list(sums)).values():
        total += value
    total += meet({j: come[j] for j in (two, one)}, order, grads)
    total, come = hold((total, come))
    total += meet({j: come[j] for j in late}, order, grads)
    mine, layers = total[0], lax.axis_size("layer")
    if layers & (layers - 1) or layers > 4:
        return lax.psum(mine, "layer")
    for j in range(1, layers):
        total += lax.ppermute(mine, "layer", [(s, s ^ j) for s in range(layers)])
    return total[0]


def solution(mesh):
    placed = (
        P("layer", "seq", None),
        P("layer", "seq", None),
        P("layer", "seq", None),
        P("layer", None, None, None),
        P("layer", "seq", None, None),
        P("layer", None),
    )
    across = mesh.shape["seq"] // LINE
    return jax.shard_map(
        functools.partial(body, across), mesh=mesh, in_specs=placed, out_specs=P("seq"), check_vma=False
    )
```

```python
import functools

import jax
import jax.numpy as jnp
from jax import lax
from jax.experimental import pallas as pl
from jax.experimental.pallas import tpu as pltpu
from jax.sharding import PartitionSpec as P

LINE = 4
TILE = 128
MIB = 2**20
NT = (((1,), (1,)), ((), ()))
hold = lax.optimization_barrier
free = pl.CostEstimate(flops=0, bytes_accessed=0, transcendentals=0)


def blocks_of(wide):
    return [pl.ds(n * TILE, TILE) for n in range(wide // TILE)]


def project_kernel(count, *refs):
    chunks, (basis, query, out, turned) = refs[:count], refs[count:]
    rows = chunks[0].shape[0]

    @pl.when(pl.program_id(0) == 0)
    def _():
        for c, chunk in enumerate(chunks):
            for n, part in enumerate(blocks_of(turned.shape[1])):
                turned[pl.ds(c * rows, rows), part] = jnp.dot(
                    chunk[:, part], basis[n], preferred_element_type=jnp.float32
                ).astype(jnp.bfloat16)

    found = lax.dot_general(turned[...], query[...], NT, preferred_element_type=jnp.float32)
    out[...] = found.reshape(out.shape)


def project(chunks, basis, query):
    count, rows = len(chunks), chunks[0].shape[0]
    units, wide = query.shape
    step = 2 * TILE if units % (2 * TILE) == 0 else TILE
    whole = lambda *shape: pl.BlockSpec(shape, lambda i: (0,) * len(shape))
    return pl.pallas_call(
        functools.partial(project_kernel, count),
        grid=(units // step,),
        in_specs=[whole(rows, wide)] * count + [whole(*basis.shape), pl.BlockSpec((step, wide), lambda i: (i, 0))],
        out_specs=pl.BlockSpec((count, rows, step), lambda i: (0, 0, i)),
        out_shape=jax.ShapeDtypeStruct((count, rows, units), jnp.float32),
        scratch_shapes=[pltpu.VMEM((count * rows, wide), jnp.bfloat16)],
        compiler_params=pltpu.CompilerParams(vmem_limit_bytes=20 * MIB),
        cost_estimate=free,
    )(*chunks, basis, query)


def pack_kernel(count, order, *refs):
    for piece, out in zip(refs[:count], refs[count:]):
        out[...] = piece[...]


def pack(offsets, order, grads, units):
    rows, count = grads.shape[0], len(offsets)
    found = pl.pallas_call(
        functools.partial(pack_kernel, count),
        grid_spec=pltpu.PrefetchScalarGridSpec(
            num_scalar_prefetch=1,
            grid=(1,),
            in_specs=[pl.BlockSpec((rows, units), lambda i, order, j=j: (0, order[j])) for j in offsets],
            out_specs=[pl.BlockSpec((rows, units), lambda i, order: (0, 0))] * count,
        ),
        out_shape=[jax.ShapeDtypeStruct((rows, units), grads.dtype)] * count,
        compiler_params=pltpu.CompilerParams(vmem_limit_bytes=16 * MIB),
        cost_estimate=free,
    )(order, *[grads] * count)
    return dict(zip(offsets, found))


def lay(total):
    return jnp.sum(total.T, axis=0, keepdims=True)


def score_kernel(order, found, piece, basis, out):
    total = jnp.zeros((piece.shape[0], TILE), jnp.float32)
    for n, part in enumerate(blocks_of(piece.shape[1])):
        turned = jnp.dot(piece[:, part], basis[n], preferred_element_type=jnp.float32).astype(jnp.bfloat16)
        total += turned.astype(jnp.float32) * found[:, part]
    out[...] = lay(total)


def meet_kernel(count, order, *refs):
    total = jnp.zeros((refs[0].shape[0], TILE), jnp.float32)
    for came, piece in zip(refs[:count], refs[count:-1]):
        for part in blocks_of(piece.shape[1]):
            total += came[:, part].astype(jnp.float32) * piece[:, part].astype(jnp.float32)
    refs[-1][...] = lay(total)


def small(kernel, order, in_specs, rows, *args):
    return pl.pallas_call(
        kernel,
        grid_spec=pltpu.PrefetchScalarGridSpec(
            num_scalar_prefetch=1,
            grid=(1,),
            in_specs=in_specs,
            out_specs=pl.BlockSpec((1, rows), lambda i, order: (0, 0)),
        ),
        out_shape=jax.ShapeDtypeStruct((1, rows), jnp.float32),
        compiler_params=pltpu.CompilerParams(vmem_limit_bytes=16 * MIB),
        cost_estimate=free,
    )(order, *args)


def score(found, c, order, j, values, basis):
    _, rows, units = found.shape
    at = (lambda i, order: (0, 0)) if j is None else (lambda i, order: (0, order[j]))
    specs = [
        pl.BlockSpec((None, rows, units), lambda i, order: (c, 0, 0)),
        pl.BlockSpec((rows, units), at),
        pl.BlockSpec(basis.shape, lambda i, order: (0, 0, 0)),
    ]
    return small(score_kernel, order, specs, rows, found, values, basis)


def meet(come, order, grads):
    offsets = list(come)
    rows, units = come[offsets[0]].shape
    specs = [pl.BlockSpec((rows, units), lambda i, order: (0, 0))] * len(offsets)
    specs += [pl.BlockSpec((rows, units), lambda i, order, j=j: (0, order[j])) for j in offsets]
    args = [come[j] for j in offsets] + [grads] * len(offsets)
    return small(functools.partial(meet_kernel, len(offsets)), order, specs, rows, *args)


def back_kernel(found, basis, out):
    for n, part in enumerate(blocks_of(found.shape[1])):
        held = found[:, part]
        high = held.astype(jnp.bfloat16)
        low = (held - high.astype(jnp.float32)).astype(jnp.bfloat16)
        turned = lax.dot_general(high, basis[n], NT, preferred_element_type=jnp.float32)
        turned += lax.dot_general(low, basis[n], NT, preferred_element_type=jnp.float32)
        out[:, part] = turned.astype(jnp.bfloat16)


def back(found, c, basis):
    _, rows, units = found.shape
    return pl.pallas_call(
        back_kernel,
        grid=(1,),
        in_specs=[
            pl.BlockSpec((None, rows, units), lambda i: (c, 0, 0)),
            pl.BlockSpec(basis.shape, lambda i: (0, 0, 0)),
        ],
        out_specs=pl.BlockSpec((rows, units), lambda i: (0, 0)),
        out_shape=jax.ShapeDtypeStruct((rows, units), jnp.bfloat16),
        compiler_params=pltpu.CompilerParams(vmem_limit_bytes=16 * MIB),
        cost_estimate=free,
    )(found, basis)


def joined_kernel(wide, found, first, second, basis, out):
    ends = [(held, n) for held in (first, second) for n in range(wide, held.shape[1], TILE)]
    total = jnp.zeros((found.shape[0], TILE), jnp.float32)
    for n, (held, at) in enumerate(ends):
        piece = held[:, pl.ds(at, TILE)]
        turned = jnp.dot(piece, basis[n], preferred_element_type=jnp.float32).astype(jnp.bfloat16)
        total += turned.astype(jnp.float32) * found[:, pl.ds(n * TILE, TILE)]
    out[...] = lay(total)


def score_joined(found, c, first, second, wide, basis):
    _, rows, units = found.shape
    return pl.pallas_call(
        functools.partial(joined_kernel, wide),
        grid=(1,),
        in_specs=[
            pl.BlockSpec((None, rows, units), lambda i: (c, 0, 0)),
            pl.BlockSpec(first.shape, lambda i: (0, 0)),
            pl.BlockSpec(second.shape, lambda i: (0, 0)),
            pl.BlockSpec(basis.shape, lambda i: (0, 0, 0)),
        ],
        out_specs=pl.BlockSpec((1, rows), lambda i: (0, 0)),
        out_shape=jax.ShapeDtypeStruct((1, rows), jnp.float32),
        compiler_params=pltpu.CompilerParams(vmem_limit_bytes=16 * MIB),
        cost_estimate=free,
    )(found, first, second, basis)


def project_score_kernel(chunk, basis, query, piece, turn, out, turned, total):
    @pl.when(pl.program_id(0) == 0)
    def _():
        for n, part in enumerate(blocks_of(chunk.shape[1])):
            turned[:, part] = jnp.dot(chunk[:, part], basis[n], preferred_element_type=jnp.float32).astype(jnp.bfloat16)
        total[...] = jnp.zeros_like(total)

    found = lax.dot_general(turned[...], query[...], NT, preferred_element_type=jnp.float32)
    for n in range(turn.shape[0]):
        part = slice(n * TILE, (n + 1) * TILE)
        held = jnp.dot(piece[:, part], turn[n], preferred_element_type=jnp.float32).astype(jnp.bfloat16)
        total[...] += held.astype(jnp.float32) * found[:, part]

    @pl.when(pl.program_id(0) == pl.num_programs(0) - 1)
    def _():
        out[...] = lay(total[...])


def project_score(chunk, basis, query, piece, turn):
    rows, wide = chunk.shape
    units = query.shape[0]
    step = 2 * TILE if units % (2 * TILE) == 0 else TILE
    whole = lambda *shape: pl.BlockSpec(shape, lambda i: (0,) * len(shape))
    return pl.pallas_call(
        project_score_kernel,
        grid=(units // step,),
        in_specs=[
            whole(rows, wide),
            whole(*basis.shape),
            pl.BlockSpec((step, wide), lambda i: (i, 0)),
            pl.BlockSpec((rows, step), lambda i: (0, i)),
            pl.BlockSpec((step // TILE, *turn.shape[1:]), lambda i: (i, 0, 0)),
        ],
        out_specs=whole(1, rows),
        out_shape=jax.ShapeDtypeStruct((1, rows), jnp.float32),
        scratch_shapes=[pltpu.VMEM((rows, wide), jnp.bfloat16), pltpu.VMEM((rows, TILE), jnp.float32)],
        compiler_params=pltpu.CompilerParams(vmem_limit_bytes=20 * MIB),
        cost_estimate=free,
    )(chunk, basis, query, piece, turn)


def body(across, train_inputs, out_grads, query_blocks, basis_in, basis_out, block_of):
    own, grads, query = train_inputs[0], out_grads[0], query_blocks[0]
    turn_in, turn_out, owners = basis_in[0], basis_out[0], block_of[0]
    size, units = LINE * across, query.shape[0]
    me = lax.axis_index("seq")
    inner = (me // across == 1) | (me // across == 2)
    order = jnp.take(owners, jnp.arange(size) ^ me)

    def move(value, place):
        pairs = []
        for s in range(size):
            to = place(s // across, s % across)
            if to is not None:
                pairs.append((s, to[0] * across + to[1]))
        return lax.ppermute(value, "seq", pairs)

    def swap(value, j):
        return lax.ppermute(value, "seq", [(s, s ^ j) for s in range(size)])

    def sideways(value):
        return [swap(value, j) for j in range(1, across)]

    middle = lambda value: move(value, lambda z, x: (3 - z, x) if z in (1, 2) else None)
    line = lambda value, d: swap(value, d * across)
    send = lambda values, js: {j: swap(values[j], j) for j in js}
    aside = lambda d: [d * across + j for j in range(1, across)]
    one, two, three = across, 2 * across, 3 * across

    wide, cut = own.shape[1], units // TILE // 2 * TILE
    got, come = {}, {}
    a1, a2, a3 = line(own, 1), middle(own), sideways(own)
    pieces = pack(aside(0) + [three] + aside(3), order, grads, units)
    p_own = project([own], turn_in, query)
    a1, pieces, p_own = hold((a1, pieces, p_own))
    join = lambda value, cols: [swap(jnp.concatenate([value, pieces[j][:, cols]], axis=1), j) for j in range(1, across)]
    got.update(send(pieces, aside(3)))
    b1, b2 = middle(a1), line(a2, 1)
    b3 = join(a1, slice(0, cut))
    total = score(p_own, 0, order, 0, grads, turn_out)
    a1, a3, a2, b1, b2, pieces, total = hold((a1, a3, a2, b1, b2, pieces, total))
    c1 = line(b1, 1)
    far2 = jnp.where(inner, b1, b2)
    side2 = join(far2, slice(cut, units))
    got.update(send(pieces, [three]))
    p_a = project([a1] + a3, turn_in, query)
    ready = {one: back(p_a, 0, turn_out)}
    p_b = project([far2] + b3, turn_in, query)
    ready[two] = back(p_b, 0, turn_out)
    for j in range(1, across):
        ready[one + j] = back(p_b, j, turn_out)
    c1, got, ready = hold((c1, got, ready))
    far3 = jnp.where(inner, a2, c1)
    side3 = sideways(far3)
    come.update(send(ready, [two, one]))
    p_c = project([far3] + side2, turn_in, query)
    sums = {three: score(p_c, 0, order, None, got[three], turn_out)}
    for j in range(1, across):
        ready[two + j] = back(p_c, j, turn_out)
        sums[j] = score_joined(p_a, j, b3[j - 1], side2[j - 1], wide, turn_out)
    for value in send(sums, list(sums)).values():
        total += value
    side3, ready, total, come = hold((side3, ready, total, come))
    late = aside(2) + aside(1)
    come.update(send(ready, late))
    sums = {}
    for j in range(1, across):
        sums[three + j] = project_score(side3[j - 1], turn_in, query, got[three + j], turn_out)
    for value in send(sums, list(sums)).values():
        total += value
    total += meet({j: come[j] for j in (two, one)}, order, grads)
    total, come = hold((total, come))
    total += meet({j: come[j] for j in late}, order, grads)
    mine, layers = total[0], lax.axis_size("layer")
    if layers & (layers - 1) or layers > 4:
        return lax.psum(mine, "layer")
    for j in range(1, layers):
        total += lax.ppermute(mine, "layer", [(s, s ^ j) for s in range(layers)])
    return total[0]


def solution(mesh):
    placed = (
        P("layer", "seq", None),
        P("layer", "seq", None),
        P("layer", "seq", None),
        P("layer", None, None, None),
        P("layer", "seq", None, None),
        P("layer", None),
    )
    across = mesh.shape["seq"] // LINE
    return jax.shard_map(
        functools.partial(body, across), mesh=mesh, in_specs=placed, out_specs=P("seq"), check_vma=False
    )
```

```python
import functools

import jax
import jax.numpy as jnp
from jax import lax
from jax.experimental import pallas as pl
from jax.experimental.pallas import tpu as pltpu
from jax.sharding import PartitionSpec as P

LINE = 4
TILE = 128
MIB = 2**20
NT = (((1,), (1,)), ((), ()))
hold = lax.optimization_barrier
free = pl.CostEstimate(flops=0, bytes_accessed=0, transcendentals=0)


def blocks_of(wide):
    return [pl.ds(n * TILE, TILE) for n in range(wide // TILE)]


def project_kernel(count, *refs):
    chunks, (basis, query, out, turned) = refs[:count], refs[count:]
    rows = chunks[0].shape[0]

    @pl.when(pl.program_id(0) == 0)
    def _():
        for c, chunk in enumerate(chunks):
            for n, part in enumerate(blocks_of(turned.shape[1])):
                turned[pl.ds(c * rows, rows), part] = jnp.dot(
                    chunk[:, part], basis[n], preferred_element_type=jnp.float32
                ).astype(jnp.bfloat16)

    found = lax.dot_general(turned[...], query[...], NT, preferred_element_type=jnp.float32)
    out[...] = found.reshape(out.shape)


def project(chunks, basis, query):
    count, rows = len(chunks), chunks[0].shape[0]
    units, wide = query.shape
    step = 2 * TILE if units % (2 * TILE) == 0 else TILE
    whole = lambda *shape: pl.BlockSpec(shape, lambda i: (0,) * len(shape))
    return pl.pallas_call(
        functools.partial(project_kernel, count),
        grid=(units // step,),
        in_specs=[whole(rows, wide)] * count + [whole(*basis.shape), pl.BlockSpec((step, wide), lambda i: (i, 0))],
        out_specs=pl.BlockSpec((count, rows, step), lambda i: (0, 0, i)),
        out_shape=jax.ShapeDtypeStruct((count, rows, units), jnp.float32),
        scratch_shapes=[pltpu.VMEM((count * rows, wide), jnp.bfloat16)],
        compiler_params=pltpu.CompilerParams(vmem_limit_bytes=20 * MIB),
        cost_estimate=free,
    )(*chunks, basis, query)


def pack_kernel(count, order, *refs):
    for piece, out in zip(refs[:count], refs[count:]):
        out[...] = piece[...]


def pack(offsets, order, grads, units):
    rows, count = grads.shape[0], len(offsets)
    found = pl.pallas_call(
        functools.partial(pack_kernel, count),
        grid_spec=pltpu.PrefetchScalarGridSpec(
            num_scalar_prefetch=1,
            grid=(1,),
            in_specs=[pl.BlockSpec((rows, units), lambda i, order, j=j: (0, order[j])) for j in offsets],
            out_specs=[pl.BlockSpec((rows, units), lambda i, order: (0, 0))] * count,
        ),
        out_shape=[jax.ShapeDtypeStruct((rows, units), grads.dtype)] * count,
        compiler_params=pltpu.CompilerParams(vmem_limit_bytes=16 * MIB),
        cost_estimate=free,
    )(order, *[grads] * count)
    return dict(zip(offsets, found))


def lay(total):
    return jnp.sum(total.T, axis=0, keepdims=True)


def score_kernel(order, found, piece, basis, out):
    total = jnp.zeros((piece.shape[0], TILE), jnp.float32)
    for n, part in enumerate(blocks_of(piece.shape[1])):
        turned = jnp.dot(piece[:, part], basis[n], preferred_element_type=jnp.float32).astype(jnp.bfloat16)
        total += turned.astype(jnp.float32) * found[:, part]
    out[...] = lay(total)


def meet_kernel(count, *refs):
    total = jnp.zeros((refs[0].shape[0], TILE), jnp.float32)
    for came, piece in zip(refs[:count], refs[count:-1]):
        for part in blocks_of(piece.shape[1]):
            total += came[:, part].astype(jnp.float32) * piece[:, part].astype(jnp.float32)
    refs[-1][...] = lay(total)


def small(kernel, order, in_specs, rows, *args):
    return pl.pallas_call(
        kernel,
        grid_spec=pltpu.PrefetchScalarGridSpec(
            num_scalar_prefetch=1,
            grid=(1,),
            in_specs=in_specs,
            out_specs=pl.BlockSpec((1, rows), lambda i, order: (0, 0)),
        ),
        out_shape=jax.ShapeDtypeStruct((1, rows), jnp.float32),
        compiler_params=pltpu.CompilerParams(vmem_limit_bytes=16 * MIB),
        cost_estimate=free,
    )(order, *args)


def score(found, c, order, j, values, basis):
    _, rows, units = found.shape
    at = (lambda i, order: (0, 0)) if j is None else (lambda i, order: (0, order[j]))
    specs = [
        pl.BlockSpec((None, rows, units), lambda i, order: (c, 0, 0)),
        pl.BlockSpec((rows, units), at),
        pl.BlockSpec(basis.shape, lambda i, order: (0, 0, 0)),
    ]
    return small(score_kernel, order, specs, rows, found, values, basis)


def meet(come, pieces):
    offsets = list(come)
    vmem = pl.BlockSpec(memory_space=pltpu.VMEM)
    return pl.pallas_call(
        functools.partial(meet_kernel, len(offsets)),
        in_specs=[vmem] * (2 * len(offsets)),
        out_specs=vmem,
        out_shape=jax.ShapeDtypeStruct((1, pieces[offsets[0]].shape[0]), jnp.float32),
        compiler_params=pltpu.CompilerParams(vmem_limit_bytes=16 * MIB),
        cost_estimate=free,
    )(*[come[j] for j in offsets], *[pieces[j] for j in offsets])


def back_kernel(found, basis, out):
    for n, part in enumerate(blocks_of(found.shape[1])):
        held = found[:, part]
        high = held.astype(jnp.bfloat16)
        low = (held - high.astype(jnp.float32)).astype(jnp.bfloat16)
        turned = lax.dot_general(high, basis[n], NT, preferred_element_type=jnp.float32)
        turned += lax.dot_general(low, basis[n], NT, preferred_element_type=jnp.float32)
        out[:, part] = turned.astype(jnp.bfloat16)


def back(found, c, basis):
    _, rows, units = found.shape
    return pl.pallas_call(
        back_kernel,
        grid=(1,),
        in_specs=[
            pl.BlockSpec((None, rows, units), lambda i: (c, 0, 0)),
            pl.BlockSpec(basis.shape, lambda i: (0, 0, 0)),
        ],
        out_specs=pl.BlockSpec((rows, units), lambda i: (0, 0)),
        out_shape=jax.ShapeDtypeStruct((rows, units), jnp.bfloat16),
        compiler_params=pltpu.CompilerParams(vmem_limit_bytes=16 * MIB),
        cost_estimate=free,
    )(found, basis)


def joined_kernel(wide, found, first, second, basis, out):
    ends = [(held, n) for held in (first, second) for n in range(wide, held.shape[1], TILE)]
    total = jnp.zeros((found.shape[0], TILE), jnp.float32)
    for n, (held, at) in enumerate(ends):
        piece = held[:, pl.ds(at, TILE)]
        turned = jnp.dot(piece, basis[n], preferred_element_type=jnp.float32).astype(jnp.bfloat16)
        total += turned.astype(jnp.float32) * found[:, pl.ds(n * TILE, TILE)]
    out[...] = lay(total)


def score_joined(found, c, first, second, wide, basis):
    _, rows, units = found.shape
    return pl.pallas_call(
        functools.partial(joined_kernel, wide),
        grid=(1,),
        in_specs=[
            pl.BlockSpec((None, rows, units), lambda i: (c, 0, 0)),
            pl.BlockSpec(first.shape, lambda i: (0, 0)),
            pl.BlockSpec(second.shape, lambda i: (0, 0)),
            pl.BlockSpec(basis.shape, lambda i: (0, 0, 0)),
        ],
        out_specs=pl.BlockSpec((1, rows), lambda i: (0, 0)),
        out_shape=jax.ShapeDtypeStruct((1, rows), jnp.float32),
        compiler_params=pltpu.CompilerParams(vmem_limit_bytes=16 * MIB),
        cost_estimate=free,
    )(found, first, second, basis)


def project_score_kernel(chunk, basis, query, piece, turn, out, turned, total):
    @pl.when(pl.program_id(0) == 0)
    def _():
        for n, part in enumerate(blocks_of(chunk.shape[1])):
            turned[:, part] = jnp.dot(chunk[:, part], basis[n], preferred_element_type=jnp.float32).astype(jnp.bfloat16)
        total[...] = jnp.zeros_like(total)

    found = lax.dot_general(turned[...], query[...], NT, preferred_element_type=jnp.float32)
    for n in range(turn.shape[0]):
        part = slice(n * TILE, (n + 1) * TILE)
        held = jnp.dot(piece[:, part], turn[n], preferred_element_type=jnp.float32).astype(jnp.bfloat16)
        total[...] += held.astype(jnp.float32) * found[:, part]

    @pl.when(pl.program_id(0) == pl.num_programs(0) - 1)
    def _():
        out[...] = lay(total[...])


def project_score(chunk, basis, query, piece, turn):
    rows, wide = chunk.shape
    units = query.shape[0]
    step = 2 * TILE if units % (2 * TILE) == 0 else TILE
    whole = lambda *shape: pl.BlockSpec(shape, lambda i: (0,) * len(shape))
    return pl.pallas_call(
        project_score_kernel,
        grid=(units // step,),
        in_specs=[
            whole(rows, wide),
            whole(*basis.shape),
            pl.BlockSpec((step, wide), lambda i: (i, 0)),
            pl.BlockSpec((rows, step), lambda i: (0, i)),
            pl.BlockSpec((step // TILE, *turn.shape[1:]), lambda i: (i, 0, 0)),
        ],
        out_specs=whole(1, rows),
        out_shape=jax.ShapeDtypeStruct((1, rows), jnp.float32),
        scratch_shapes=[pltpu.VMEM((rows, wide), jnp.bfloat16), pltpu.VMEM((rows, TILE), jnp.float32)],
        compiler_params=pltpu.CompilerParams(vmem_limit_bytes=20 * MIB),
        cost_estimate=free,
    )(chunk, basis, query, piece, turn)


def body(across, train_inputs, out_grads, query_blocks, basis_in, basis_out, block_of):
    own, grads, query = train_inputs[0], out_grads[0], query_blocks[0]
    turn_in, turn_out, owners = basis_in[0], basis_out[0], block_of[0]
    size, units = LINE * across, query.shape[0]
    me = lax.axis_index("seq")
    inner = (me // across == 1) | (me // across == 2)
    order = jnp.take(owners, jnp.arange(size) ^ me)

    def move(value, place):
        pairs = []
        for s in range(size):
            to = place(s // across, s % across)
            if to is not None:
                pairs.append((s, to[0] * across + to[1]))
        return lax.ppermute(value, "seq", pairs)

    def swap(value, j):
        return lax.ppermute(value, "seq", [(s, s ^ j) for s in range(size)])

    def sideways(value):
        return [swap(value, j) for j in range(1, across)]

    middle = lambda value: move(value, lambda z, x: (3 - z, x) if z in (1, 2) else None)
    line = lambda value, d: swap(value, d * across)
    send = lambda values, js: {j: swap(values[j], j) for j in js}
    aside = lambda d: [d * across + j for j in range(1, across)]
    one, two, three = across, 2 * across, 3 * across

    wide, cut = own.shape[1], units // TILE // 2 * TILE
    got, come = {}, {}
    a1, a2, a3 = line(own, 1), middle(own), sideways(own)
    pieces = pack(list(range(1, size)), order, grads, units)
    p_own = project([own], turn_in, query)
    a1, pieces, p_own = hold((a1, pieces, p_own))
    join = lambda value, cols: [swap(jnp.concatenate([value, pieces[j][:, cols]], axis=1), j) for j in range(1, across)]
    got.update(send(pieces, aside(3)))
    b1, b2 = middle(a1), line(a2, 1)
    b3 = join(a1, slice(0, cut))
    total = score(p_own, 0, order, 0, grads, turn_out)
    a1, a3, a2, b1, b2, pieces, total = hold((a1, a3, a2, b1, b2, pieces, total))
    c1 = line(b1, 1)
    far2 = jnp.where(inner, b1, b2)
    side2 = join(far2, slice(cut, units))
    got.update(send(pieces, [three]))
    p_a = project([a1] + a3, turn_in, query)
    ready = {one: back(p_a, 0, turn_out)}
    p_b = project([far2] + b3, turn_in, query)
    ready[two] = back(p_b, 0, turn_out)
    for j in range(1, across):
        ready[one + j] = back(p_b, j, turn_out)
    c1, got, ready = hold((c1, got, ready))
    far3 = jnp.where(inner, a2, c1)
    side3 = sideways(far3)
    come.update(send(ready, [two, one]))
    p_c = project([far3] + side2, turn_in, query)
    sums = {three: score(p_c, 0, order, None, got[three], turn_out)}
    for j in range(1, across):
        ready[two + j] = back(p_c, j, turn_out)
        sums[j] = score_joined(p_a, j, b3[j - 1], side2[j - 1], wide, turn_out)
    for value in send(sums, list(sums)).values():
        total += value
    side3, ready, total, come = hold((side3, ready, total, come))
    late = aside(2) + aside(1)
    come.update(send(ready, late))
    sums = {}
    for j in range(1, across):
        sums[three + j] = project_score(side3[j - 1], turn_in, query, got[three + j], turn_out)
    for value in send(sums, list(sums)).values():
        total += value
    total += meet({j: come[j] for j in (two, one)}, pieces)
    total, come = hold((total, come))
    total += meet({j: come[j] for j in late}, pieces)
    mine, layers = total[0], lax.axis_size("layer")
    if layers & (layers - 1) or layers > 4:
        return lax.psum(mine, "layer")
    for j in range(1, layers):
        total += lax.ppermute(mine, "layer", [(s, s ^ j) for s in range(layers)])
    return total[0]


def solution(mesh):
    placed = (
        P("layer", "seq", None),
        P("layer", "seq", None),
        P("layer", "seq", None),
        P("layer", None, None, None),
        P("layer", "seq", None, None),
        P("layer", None),
    )
    across = mesh.shape["seq"] // LINE
    return jax.shard_map(
        functools.partial(body, across), mesh=mesh, in_specs=placed, out_specs=P("seq"), check_vma=False
    )
```

```python
import functools

import jax
import jax.numpy as jnp
from jax import lax
from jax.experimental import pallas as pl
from jax.experimental.pallas import tpu as pltpu
from jax.sharding import PartitionSpec as P

LINE = 4
TILE = 128
MIB = 2**20
NT = (((1,), (1,)), ((), ()))
hold = lax.optimization_barrier
free = pl.CostEstimate(flops=0, bytes_accessed=0, transcendentals=0)


def blocks_of(wide):
    return [pl.ds(n * TILE, TILE) for n in range(wide // TILE)]


def project_kernel(count, *refs):
    chunks, (basis, query, out, turned) = refs[:count], refs[count:]
    rows = chunks[0].shape[0]

    @pl.when(pl.program_id(0) == 0)
    def _():
        for c, chunk in enumerate(chunks):
            for n, part in enumerate(blocks_of(turned.shape[1])):
                turned[pl.ds(c * rows, rows), part] = jnp.dot(
                    chunk[:, part], basis[n], preferred_element_type=jnp.float32
                ).astype(jnp.bfloat16)

    found = lax.dot_general(turned[...], query[...], NT, preferred_element_type=jnp.float32)
    out[...] = found.reshape(out.shape)


def project(chunks, basis, query):
    count, rows = len(chunks), chunks[0].shape[0]
    units, wide = query.shape
    step = 2 * TILE if units % (2 * TILE) == 0 else TILE
    whole = lambda *shape: pl.BlockSpec(shape, lambda i: (0,) * len(shape))
    return pl.pallas_call(
        functools.partial(project_kernel, count),
        grid=(units // step,),
        in_specs=[whole(rows, wide)] * count + [whole(*basis.shape), pl.BlockSpec((step, wide), lambda i: (i, 0))],
        out_specs=pl.BlockSpec((count, rows, step), lambda i: (0, 0, i)),
        out_shape=jax.ShapeDtypeStruct((count, rows, units), jnp.float32),
        scratch_shapes=[pltpu.VMEM((count * rows, wide), jnp.bfloat16)],
        compiler_params=pltpu.CompilerParams(vmem_limit_bytes=20 * MIB),
        cost_estimate=free,
    )(*chunks, basis, query)


def pack_kernel(count, order, *refs):
    for piece, out in zip(refs[:count], refs[count:]):
        out[...] = piece[...]


def pack(offsets, order, grads, units):
    rows, count = grads.shape[0], len(offsets)
    found = pl.pallas_call(
        functools.partial(pack_kernel, count),
        grid_spec=pltpu.PrefetchScalarGridSpec(
            num_scalar_prefetch=1,
            grid=(1,),
            in_specs=[pl.BlockSpec((rows, units), lambda i, order, j=j: (0, order[j])) for j in offsets],
            out_specs=[pl.BlockSpec((rows, units), lambda i, order: (0, 0))] * count,
        ),
        out_shape=[jax.ShapeDtypeStruct((rows, units), grads.dtype)] * count,
        compiler_params=pltpu.CompilerParams(vmem_limit_bytes=16 * MIB),
        cost_estimate=free,
    )(order, *[grads] * count)
    return dict(zip(offsets, found))


def lay(total):
    return jnp.sum(total.T, axis=0, keepdims=True)


def score_kernel(order, found, piece, basis, out):
    total = jnp.zeros((piece.shape[0], TILE), jnp.float32)
    for n, part in enumerate(blocks_of(piece.shape[1])):
        turned = jnp.dot(piece[:, part], basis[n], preferred_element_type=jnp.float32).astype(jnp.bfloat16)
        total += turned.astype(jnp.float32) * found[:, part]
    out[...] = lay(total)


def meet_kernel(count, *refs):
    total = jnp.zeros((refs[0].shape[0], TILE), jnp.float32)
    for came, piece in zip(refs[:count], refs[count:-1]):
        for part in blocks_of(piece.shape[1]):
            total += came[:, part].astype(jnp.float32) * piece[:, part].astype(jnp.float32)
    refs[-1][...] = lay(total)


def small(kernel, order, in_specs, rows, *args):
    return pl.pallas_call(
        kernel,
        grid_spec=pltpu.PrefetchScalarGridSpec(
            num_scalar_prefetch=1,
            grid=(1,),
            in_specs=in_specs,
            out_specs=pl.BlockSpec((1, rows), lambda i, order: (0, 0)),
        ),
        out_shape=jax.ShapeDtypeStruct((1, rows), jnp.float32),
        compiler_params=pltpu.CompilerParams(vmem_limit_bytes=16 * MIB),
        cost_estimate=free,
    )(order, *args)


def score(found, c, order, j, values, basis):
    _, rows, units = found.shape
    at = (lambda i, order: (0, 0)) if j is None else (lambda i, order: (0, order[j]))
    specs = [
        pl.BlockSpec((None, rows, units), lambda i, order: (c, 0, 0)),
        pl.BlockSpec((rows, units), at),
        pl.BlockSpec(basis.shape, lambda i, order: (0, 0, 0)),
    ]
    return small(score_kernel, order, specs, rows, found, values, basis)


def meet(come, pieces):
    offsets = list(come)
    vmem = pl.BlockSpec(memory_space=pltpu.VMEM)
    return pl.pallas_call(
        functools.partial(meet_kernel, len(offsets)),
        in_specs=[vmem] * (2 * len(offsets)),
        out_specs=vmem,
        out_shape=jax.ShapeDtypeStruct((1, pieces[offsets[0]].shape[0]), jnp.float32),
        compiler_params=pltpu.CompilerParams(vmem_limit_bytes=16 * MIB),
        cost_estimate=free,
    )(*[come[j] for j in offsets], *[pieces[j] for j in offsets])


def back_kernel(found, basis, out):
    for n, part in enumerate(blocks_of(found.shape[1])):
        held = found[:, part]
        high = held.astype(jnp.bfloat16)
        low = (held - high.astype(jnp.float32)).astype(jnp.bfloat16)
        turned = lax.dot_general(high, basis[n], NT, preferred_element_type=jnp.float32)
        turned += lax.dot_general(low, basis[n], NT, preferred_element_type=jnp.float32)
        out[:, part] = turned.astype(jnp.bfloat16)


def back(found, c, basis):
    _, rows, units = found.shape
    return pl.pallas_call(
        back_kernel,
        grid=(1,),
        in_specs=[
            pl.BlockSpec((None, rows, units), lambda i: (c, 0, 0)),
            pl.BlockSpec(basis.shape, lambda i: (0, 0, 0)),
        ],
        out_specs=pl.BlockSpec((rows, units), lambda i: (0, 0)),
        out_shape=jax.ShapeDtypeStruct((rows, units), jnp.bfloat16),
        compiler_params=pltpu.CompilerParams(vmem_limit_bytes=16 * MIB),
        cost_estimate=free,
    )(found, basis)


def joined_kernel(wide, found, first, second, basis, out):
    ends = [(held, n) for held in (first, second) for n in range(wide, held.shape[1], TILE)]
    total = jnp.zeros((found.shape[0], TILE), jnp.float32)
    for n, (held, at) in enumerate(ends):
        piece = held[:, pl.ds(at, TILE)]
        turned = jnp.dot(piece, basis[n], preferred_element_type=jnp.float32).astype(jnp.bfloat16)
        total += turned.astype(jnp.float32) * found[:, pl.ds(n * TILE, TILE)]
    out[...] = lay(total)


def score_joined(found, c, first, second, wide, basis):
    _, rows, units = found.shape
    return pl.pallas_call(
        functools.partial(joined_kernel, wide),
        grid=(1,),
        in_specs=[
            pl.BlockSpec((None, rows, units), lambda i: (c, 0, 0)),
            pl.BlockSpec(first.shape, lambda i: (0, 0)),
            pl.BlockSpec(second.shape, lambda i: (0, 0)),
            pl.BlockSpec(basis.shape, lambda i: (0, 0, 0)),
        ],
        out_specs=pl.BlockSpec((1, rows), lambda i: (0, 0)),
        out_shape=jax.ShapeDtypeStruct((1, rows), jnp.float32),
        compiler_params=pltpu.CompilerParams(vmem_limit_bytes=16 * MIB),
        cost_estimate=free,
    )(found, first, second, basis)


def project_score_kernel(chunk, basis, query, piece, turn, out, turned, total):
    @pl.when(pl.program_id(0) == 0)
    def _():
        for n, part in enumerate(blocks_of(chunk.shape[1])):
            turned[:, part] = jnp.dot(chunk[:, part], basis[n], preferred_element_type=jnp.float32).astype(jnp.bfloat16)
        total[...] = jnp.zeros_like(total)

    found = lax.dot_general(turned[...], query[...], NT, preferred_element_type=jnp.float32)
    for n in range(turn.shape[0]):
        part = slice(n * TILE, (n + 1) * TILE)
        held = jnp.dot(piece[:, part], turn[n], preferred_element_type=jnp.float32).astype(jnp.bfloat16)
        total[...] += held.astype(jnp.float32) * found[:, part]

    @pl.when(pl.program_id(0) == pl.num_programs(0) - 1)
    def _():
        out[...] = lay(total[...])


def project_score(chunk, basis, query, piece, turn):
    rows, wide = chunk.shape
    units = query.shape[0]
    step = 2 * TILE if units % (2 * TILE) == 0 else TILE
    whole = lambda *shape: pl.BlockSpec(shape, lambda i: (0,) * len(shape))
    return pl.pallas_call(
        project_score_kernel,
        grid=(units // step,),
        in_specs=[
            whole(rows, wide),
            whole(*basis.shape),
            pl.BlockSpec((step, wide), lambda i: (i, 0)),
            pl.BlockSpec((rows, step), lambda i: (0, i)),
            pl.BlockSpec((step // TILE, *turn.shape[1:]), lambda i: (i, 0, 0)),
        ],
        out_specs=whole(1, rows),
        out_shape=jax.ShapeDtypeStruct((1, rows), jnp.float32),
        scratch_shapes=[pltpu.VMEM((rows, wide), jnp.bfloat16), pltpu.VMEM((rows, TILE), jnp.float32)],
        compiler_params=pltpu.CompilerParams(vmem_limit_bytes=20 * MIB),
        cost_estimate=free,
    )(chunk, basis, query, piece, turn)


def body(across, train_inputs, out_grads, query_blocks, basis_in, basis_out, block_of):
    own, grads, query = train_inputs[0], out_grads[0], query_blocks[0]
    turn_in, turn_out, owners = basis_in[0], basis_out[0], block_of[0]
    size, units = LINE * across, query.shape[0]
    me = lax.axis_index("seq")
    inner = (me // across == 1) | (me // across == 2)
    order = jnp.take(owners, jnp.arange(size) ^ me)

    def move(value, place):
        pairs = []
        for s in range(size):
            to = place(s // across, s % across)
            if to is not None:
                pairs.append((s, to[0] * across + to[1]))
        return lax.ppermute(value, "seq", pairs)

    def swap(value, j):
        return lax.ppermute(value, "seq", [(s, s ^ j) for s in range(size)])

    def sideways(value):
        return [swap(value, j) for j in range(1, across)]

    middle = lambda value: move(value, lambda z, x: (3 - z, x) if z in (1, 2) else (z, x))
    line = lambda value, d: swap(value, d * across)
    send = lambda values, js: {j: swap(values[j], j) for j in js}
    aside = lambda d: [d * across + j for j in range(1, across)]
    one, two, three = across, 2 * across, 3 * across

    wide, cut = own.shape[1], units // TILE // 2 * TILE
    got, come = {}, {}
    a1, a2, a3 = line(own, 1), middle(own), sideways(own)
    pieces = pack(list(range(1, size)), order, grads, units)
    p_own = project([own], turn_in, query)
    a1, pieces, p_own = hold((a1, pieces, p_own))
    join = lambda value, cols: [swap(jnp.concatenate([value, pieces[j][:, cols]], axis=1), j) for j in range(1, across)]
    got.update(send(pieces, aside(3)))
    b1, b2 = middle(a1), line(a2, 1)
    b3 = join(a1, slice(0, cut))
    total = score(p_own, 0, order, 0, grads, turn_out)
    a1, a3, a2, b1, b2, pieces, total = hold((a1, a3, a2, b1, b2, pieces, total))
    c1 = line(b1, 1)
    far2 = jnp.where(inner, b1, b2)
    side2 = join(far2, slice(cut, units))
    got.update(send(pieces, [three]))
    p_a = project([a1] + a3, turn_in, query)
    ready = {one: back(p_a, 0, turn_out)}
    p_b = project([far2] + b3, turn_in, query)
    ready[two] = back(p_b, 0, turn_out)
    for j in range(1, across):
        ready[one + j] = back(p_b, j, turn_out)
    c1, got, ready = hold((c1, got, ready))
    far3 = jnp.where(inner, a2, c1)
    side3 = sideways(far3)
    come.update(send(ready, [two, one]))
    p_c = project([far3] + side2, turn_in, query)
    sums = {three: score(p_c, 0, order, None, got[three], turn_out)}
    for j in range(1, across):
        ready[two + j] = back(p_c, j, turn_out)
        sums[j] = score_joined(p_a, j, b3[j - 1], side2[j - 1], wide, turn_out)
    for value in send(sums, list(sums)).values():
        total += value
    side3, ready, total, come = hold((side3, ready, total, come))
    late = aside(2) + aside(1)
    come.update(send(ready, late))
    sums = {}
    for j in range(1, across):
        sums[three + j] = project_score(side3[j - 1], turn_in, query, got[three + j], turn_out)
    for value in send(sums, list(sums)).values():
        total += value
    total += meet({j: come[j] for j in (two, one)}, pieces)
    total, come = hold((total, come))
    total += meet({j: come[j] for j in late}, pieces)
    mine, layers = total[0], lax.axis_size("layer")
    if layers & (layers - 1) or layers > 4:
        return lax.psum(mine, "layer")
    for j in range(1, layers):
        total += lax.ppermute(mine, "layer", [(s, s ^ j) for s in range(layers)])
    return total[0]


def solution(mesh):
    placed = (
        P("layer", "seq", None),
        P("layer", "seq", None),
        P("layer", "seq", None),
        P("layer", None, None, None),
        P("layer", "seq", None, None),
        P("layer", None),
    )
    across = mesh.shape["seq"] // LINE
    return jax.shard_map(
        functools.partial(body, across), mesh=mesh, in_specs=placed, out_specs=P("seq"), check_vma=False
    )
```
